32 devices in a mesh: groups: 2 (over y), coord: 4 (over z), ex: 4 (over x, core).
Axes of the slice: x: 2, y: 2, z: 4, core: 2. Of those that a mesh axis runs over, the one named last changes fastest.
Arguments:
- gradients: bfloat16 [768, 8192], P(('groups', 'ex'), 'coord'), parts along dimension 0, may hold values from -6 to 6
- hash_salt: int32 [2], P('groups'), parts along dimension 0, may hold values from 1 to 1073741823
- slab_offset: int32 [2], P('groups'), parts along dimension 0, may hold values from 0 to 16777215
Outputs:
- features: bfloat16 [8192, 768], P('coord', ('groups', 'ex')), parts along dimension 1
- kernel: float32 [768, 384], P(('groups', 'coord'), 'ex'), parts along dimension 0
The draws below stay inside these ranges and needn't reach their ends.
There are 2 independent parts, one for each index of `groups`. The reference program is written for one: setup_inputs(seed, part) draws one part's arguments, and reference() takes and returns one part's arrays. A program takes and returns all parts, laid end to end along the dimension named above; each array names one. Nothing has to cross between parts.
All inputs are finite; a program needn't handle non-finite values.
Results may differ from the reference program's by a relative error of at most 0.0085.
Values may be sent and summed in bfloat16 or wider, within the bound.
A program may use at most 64 MiB of HBM per device.

```python
import math
import jax
import jax.numpy as jnp
from jax import lax

FEATS = 8192
COORDS = 8192
EXAMPLES = 384


def steps_of(key, shape, cuts, low, high):
    loudness = 1.0
    for dim, parts in cuts:
        heights = jax.random.uniform(jax.random.fold_in(jax.random.fold_in(key, 6), dim), (parts,), jnp.float32, low / len(cuts), high / len(cuts))
        loudness = loudness * jnp.repeat(jnp.exp(heights), shape[dim] // parts).reshape((-1,) + (1,) * (len(shape) - 1 - dim))
    return loudness


def scatter_about(own_key, extent, width, bound, cuts=(), kind=jnp.bfloat16):
    array = width * jax.random.normal(own_key, extent, jnp.float32)
    if cuts:
        array = array * steps_of(own_key, extent, cuts, -0.22, 0.18)
    return jnp.clip(array, -bound, bound).astype(kind)


def setup_inputs(seed: int = 0, part: int = 0) -> dict:
    key_of = jax.random.split(jax.random.key(seed), 4)
    part_splits = jax.random.split(jax.random.fold_in(key_of[3], part), 4)
    gradients = scatter_about(part_splits[0], (EXAMPLES, COORDS), 1.0, 6.0, ((0, 4), (1, 4)))
    hash_salt = jax.random.randint(part_splits[1], (1,), 1, 1073741824).astype(jnp.int32)
    slab_offset = jax.random.randint(part_splits[2], (1,), 0, 16777216).astype(jnp.int32)
    return dict(gradients=gradients, hash_salt=hash_salt, slab_offset=slab_offset)


def sign_block(coord_ids, first_col, block_width, salt_value):
    feature_ids = first_col + jnp.arange(block_width, dtype=jnp.int32)[:, None]
    mixed = coord_ids[None, :] * 2654435 ^ feature_ids * 97001 ^ salt_value
    mixed = mixed ^ lax.shift_right_logical(mixed, jnp.int32(15))
    mixed = mixed * 73244475
    mixed = mixed ^ lax.shift_right_logical(mixed, jnp.int32(13))
    mixed = mixed * 1274126177
    mixed = mixed ^ lax.shift_right_logical(mixed, jnp.int32(16))
    return 1 - 2 * (lax.shift_right_logical(mixed, jnp.int32(9)) & 1)

def reference(gradients, hash_salt, slab_offset):
    coords = gradients.shape[1]
    coord_ids = slab_offset[0] + jnp.arange(coords, dtype=jnp.int32)
    block_width = math.gcd(FEATS, 512)
    starts = jnp.arange(FEATS // block_width, dtype=jnp.int32) * block_width

    def one_block(first_col):
        signs = sign_block(coord_ids, first_col, block_width, hash_salt[0]).astype(jnp.bfloat16)
        return jnp.dot(signs, gradients.T, preferred_element_type=jnp.float32)
    sums = lax.map(one_block, starts).reshape(FEATS, gradients.shape[0])
    features = (sums / math.sqrt(coords)).astype(jnp.bfloat16)
    kernel = jnp.dot(features.T, features, preferred_element_type=jnp.float32) / FEATS
    return (features, kernel)
```

```python
import functools
import math

import jax
import jax.numpy as jnp
import numpy as np
from jax import lax
from jax.experimental import pallas as pl
from jax.experimental.pallas import tpu as pltpu
from jax.sharding import PartitionSpec as P

FEATS = 8192
LAST = int(np.array((1274126177 << 6) & 0xFFFFFFFF, np.uint32).astype(np.int32))


def sign_tile(coord_term, feat_term):
    m = coord_term ^ feat_term
    m = m ^ lax.shift_right_logical(m, jnp.int32(15))
    m = m * jnp.int32(73244475)
    m = m ^ lax.shift_right_logical(m, jnp.int32(13))
    p = m * jnp.int32(LAST)
    p = p ^ (p << 16)
    return jnp.where(p < 0, -1.0, 1.0).astype(jnp.bfloat16)


def project_kernel(sub, feat_rows, block, salt_ref, first_ref, place_ref, grads_ref, out_ref, signs, coord_term):
    coords = grads_ref.shape[1]
    step = pl.program_id(0)

    @pl.when(step == 0)
    def _():
        ids = first_ref[0] + lax.broadcasted_iota(jnp.int32, (16, coords), 1)
        coord_term[...] = (ids * 2654435) ^ salt_ref[0]

    @pl.loop(0, block // 16)
    def _(i):
        row = step * block + i * 16
        feat = (row // sub) * feat_rows + place_ref[0] * sub + row % sub
        feat_term = (feat + lax.broadcasted_iota(jnp.int32, (16, 128), 0)) * 97001
        for j in range(coords // 128):
            signs[pl.ds(pl.multiple_of(i * 16, 16), 16), pl.ds(j * 128, 128)] = sign_tile(
                coord_term[:, pl.ds(j * 128, 128)], feat_term
            )

    out_ref[...] = lax.dot_general(
        signs[...], grads_ref[...], (((1,), (1,)), ((), ())), preferred_element_type=jnp.float32
    ).astype(out_ref.dtype)


def project(gathered, salt, first, place, rows, sub, feat_rows):
    examples, coords = gathered.shape
    block = 512
    return pl.pallas_call(
        functools.partial(project_kernel, sub, feat_rows, block),
        grid=(rows // block,),
        out_shape=jax.ShapeDtypeStruct((rows, examples), jnp.bfloat16),
        in_specs=[pl.BlockSpec(memory_space=pltpu.SMEM)] * 3
        + [pl.BlockSpec((examples, coords), lambda i: (0, 0))],
        out_specs=pl.BlockSpec((block, examples), lambda i: (i, 0)),
        scratch_shapes=[
            pltpu.VMEM((block, coords), jnp.bfloat16),
            pltpu.VMEM((16, coords), jnp.int32),
        ],
        compiler_params=pltpu.CompilerParams(vmem_limit_bytes=40 * 2**20),
    )(salt, first, place, gathered)


def general(gradients, hash_salt, slab_offset):
    coord_local = gradients.shape[1]
    coord_parts = lax.axis_size("coord")
    ex_parts = lax.axis_size("ex")
    examples = gradients.shape[0] * ex_parts
    ex_local = gradients.shape[0]
    feat_rows = FEATS // coord_parts
    sub = feat_rows // ex_parts
    first = slab_offset + lax.axis_index("coord") * coord_local
    place = lax.axis_index("ex").reshape(1)
    gathered = lax.all_gather(gradients, "ex", axis=0, tiled=True)
    part = project(gathered, hash_salt, first, place, FEATS // ex_parts, sub, feat_rows)
    parts = lax.all_to_all(part.reshape(coord_parts, sub, examples), "coord", 0, 0)
    sums = jnp.sum(parts.astype(jnp.float32), axis=0)
    own = (sums / math.sqrt(coord_local * coord_parts)).astype(jnp.bfloat16)
    blocks = own.reshape(sub, ex_parts, ex_local).transpose(1, 0, 2)
    features = lax.all_to_all(blocks, "ex", 0, 0).reshape(feat_rows, ex_local)
    gram = lax.dot_general(own, own, (((0,), (0,)), ((), ())), preferred_element_type=jnp.float32) / FEATS
    gram = gram.astype(jnp.bfloat16).reshape(examples, ex_parts, ex_local).transpose(1, 0, 2)
    gram = jnp.sum(lax.all_to_all(gram, "ex", 0, 0).astype(jnp.float32), axis=0)
    gram = gram.astype(jnp.bfloat16).reshape(coord_parts, examples // coord_parts, ex_local)
    kernel = jnp.sum(lax.all_to_all(gram, "coord", 0, 0).astype(jnp.float32), axis=0)
    return features, kernel


def solution(mesh):
    return jax.shard_map(
        general,
        mesh=mesh,
        in_specs=(P(("groups", "ex"), "coord"), P("groups"), P("groups")),
        out_specs=(P("coord", ("groups", "ex")), P(("groups", "coord"), "ex")),
        check_vma=False,
    )
```

```python
import functools
import math

import jax
import jax.numpy as jnp
import numpy as np
from jax import lax
from jax.experimental import pallas as pl
from jax.experimental.pallas import tpu as pltpu
from jax.sharding import PartitionSpec as P

FEATS = 8192
LAST = int(np.array((1274126177 << 6) & 0xFFFFFFFF, np.uint32).astype(np.int32))


def sign_tile(coord_term, feat_term):
    m = coord_term ^ feat_term
    m = m ^ lax.shift_right_logical(m, jnp.int32(15))
    m = m * jnp.int32(73244475)
    m = m ^ lax.shift_right_logical(m, jnp.int32(13))
    p = m * jnp.int32(LAST)
    p = p ^ (p << 16)
    return jnp.where(p < 0, -1.0, 1.0).astype(jnp.bfloat16)


def project_kernel(sub, feat_rows, block, salt_ref, first_ref, place_ref, grads_ref, out_ref, signs, coord_term):
    coords = grads_ref.shape[1]
    step = pl.program_id(0)

    @pl.when(step == 0)
    def _():
        ids = first_ref[0] + lax.broadcasted_iota(jnp.int32, (16, coords), 1)
        coord_term[...] = (ids * 2654435) ^ salt_ref[0]

    @pl.loop(0, block // 16)
    def _(i):
        row = step * block + i * 16
        feat = (row // sub) * feat_rows + place_ref[0] * sub + row % sub
        feat_term = (feat + lax.broadcasted_iota(jnp.int32, (16, 128), 0)) * 97001
        for j in range(coords // 128):
            signs[pl.ds(pl.multiple_of(i * 16, 16), 16), pl.ds(j * 128, 128)] = sign_tile(
                coord_term[:, pl.ds(j * 128, 128)], feat_term
            )

    out_ref[...] = lax.dot_general(
        signs[...], grads_ref[...], (((1,), (1,)), ((), ())), preferred_element_type=jnp.float32
    ).astype(out_ref.dtype)


def project(gathered, salt, first, place, rows, sub, feat_rows):
    examples, coords = gathered.shape
    block = 512
    return pl.pallas_call(
        functools.partial(project_kernel, sub, feat_rows, block),
        grid=(rows // block,),
        out_shape=jax.ShapeDtypeStruct((rows, examples), jnp.bfloat16),
        in_specs=[pl.BlockSpec(memory_space=pltpu.SMEM)] * 3
        + [pl.BlockSpec((examples, coords), lambda i: (0, 0))],
        out_specs=pl.BlockSpec((block, examples), lambda i: (i, 0)),
        scratch_shapes=[
            pltpu.VMEM((block, coords), jnp.bfloat16),
            pltpu.VMEM((16, coords), jnp.int32),
        ],
        compiler_params=pltpu.CompilerParams(vmem_limit_bytes=40 * 2**20),
    )(salt, first, place, gathered)


def general(gradients, hash_salt, slab_offset):
    coord_local = gradients.shape[1]
    coord_parts = lax.axis_size("coord")
    ex_parts = lax.axis_size("ex")
    examples = gradients.shape[0] * ex_parts
    ex_local = gradients.shape[0]
    feat_rows = FEATS // coord_parts
    sub = feat_rows // ex_parts
    first = slab_offset + lax.axis_index("coord") * coord_local
    place = lax.axis_index("ex").reshape(1)
    gathered = lax.all_gather(gradients, "ex", axis=0, tiled=True)
    part = project(gathered, hash_salt, first, place, FEATS // ex_parts, sub, feat_rows)
    parts = lax.all_to_all(part.reshape(coord_parts, sub, examples), "coord", 0, 0)
    sums = jnp.sum(parts.astype(jnp.float32), axis=0)
    own = (sums / math.sqrt(coord_local * coord_parts)).astype(jnp.bfloat16)
    blocks = own.reshape(sub, ex_parts, ex_local).transpose(1, 0, 2)
    features = lax.all_to_all(blocks, "ex", 0, 0).reshape(feat_rows, ex_local)
    gram = lax.dot_general(own, own, (((0,), (0,)), ((), ())), preferred_element_type=jnp.float32) / FEATS
    gram = gram.astype(jnp.bfloat16).reshape(examples, ex_parts, ex_local).transpose(1, 0, 2)
    gram = jnp.sum(lax.all_to_all(gram, "ex", 0, 0).astype(jnp.float32), axis=0)
    gram = gram.astype(jnp.bfloat16).reshape(coord_parts, examples // coord_parts, ex_local)
    kernel = jnp.sum(lax.all_to_all(gram, "coord", 0, 0).astype(jnp.float32), axis=0)
    return features, kernel


def fused_kernel(
    salt_ref, offset_ref, grads_ref, feats_ref, kern_ref,
    grads, signs, coord_term, part, part_in, own, feat, feat_in, gram, gram_in,
    send_g, recv_g, send_p, recv_p, send_f, recv_f, send_k, recv_k,
):
    z, x = lax.axis_index("coord"), lax.axis_index("ex")
    xc, c = x // 2, x % 2
    zz = z % 2
    z_pair, z_far = z + 1 - 2 * zz, (z + 2) % 4
    oc, oz = 1 - c, 1 - zz
    ox = 1 - xc
    me = z * 4 + x
    n_ex, width = grads_ref.shape
    half = signs.shape[1]
    feat_rows = FEATS // 4
    sends = []

    def remote(src, dst, send, recv, zt, xt):
        return pltpu.make_async_remote_copy(
            src_ref=src, dst_ref=dst, send_sem=send, recv_sem=recv,
            device_id={"coord": zt, "ex": xt}, device_id_type=pl.DeviceIdType.MESH,
        )

    def start(*args):
        copy = remote(*args)
        copy.start()
        sends.append(copy)

    barrier = pltpu.get_barrier_semaphore()
    for d in range(1, 16):
        t = (me + d) % 16
        pl.semaphore_signal(
            barrier, inc=1, device_id={"coord": t // 4, "ex": t % 4}, device_id_type=pl.DeviceIdType.MESH
        )
    ids = offset_ref[0] + (z // 2) * (2 * width) + lax.broadcasted_iota(jnp.int32, (16, 2 * width), 1)
    coord_term[...] = (ids * 2654435) ^ salt_ref[0]
    grads[zz, xc, c] = grads_ref[...]
    pl.semaphore_wait(barrier, 15)

    mine = grads.at[zz, xc, c]
    came = recv_g.at[zz, xc, c]
    start(grads_ref, mine, send_g.at[0], came, z_pair, x)
    start(grads_ref, mine, send_g.at[1], came, z, ox * 2 + c)
    start(grads_ref, mine, send_g.at[2], came, z_pair, ox * 2 + c)
    start(grads_ref, mine, send_g.at[3], came, z, xc * 2 + oc)

    def hash_rows(low, high):
        @pl.loop(low, high)
        def _(i):
            h = i // (half // 16)
            r = i % (half // 16)
            first = ((z + 2 * h) % 4) * feat_rows + x * half + r * 16
            feat_term = (first + lax.broadcasted_iota(jnp.int32, (16, 128), 0)) * 97001
            for j in range(2 * width // 128):
                signs[h, pl.ds(pl.multiple_of(r * 16, 16), 16), pl.ds(j * 128, 128)] = sign_tile(
                    coord_term[:, pl.ds(j * 128, 128)], feat_term
                )

    def arrived(a, b, k):
        slot = grads.at[a, b, k]
        remote(slot, slot, send_g.at[0], recv_g.at[a, b, k], z_pair, x).wait_recv()

    def forward(a, b, n):
        arrived(a, b, c)
        slot = grads.at[a, b, c]
        start(slot, slot, send_g.at[n], recv_g.at[a, b, c], z, xc * 2 + oc)

    def sums(b, h):
        total = None
        for a in range(2):
            one = lax.dot_general(
                grads[a, b].reshape(2 * n_ex, width), signs[h, :, pl.ds(a * width, width)],
                (((1,), (1,)), ((), ())), preferred_element_type=jnp.float32,
            )
            total = one if total is None else total + one
        return total

    steps = half // 16
    hash_rows(0, steps)
    forward(oz, xc, 4)
    hash_rows(steps, 2 * steps)
    forward(zz, ox, 5)
    for n, b in enumerate((xc, ox)):
        if n == 0:
            arrived(zz, xc, oc)
            arrived(oz, xc, oc)
        else:
            forward(oz, ox, 6)
            arrived(zz, ox, oc)
            arrived(oz, ox, oc)
        part[n] = sums(b, 1).astype(jnp.bfloat16)
        start(part.at[n], part_in.at[n], send_p.at[n], recv_p.at[n], z_far, x)
        own[n] = sums(b, 0)

    for n, b in enumerate((xc, ox)):
        remote(part.at[n], part_in.at[n], send_p.at[n], recv_p.at[n], z_far, x).wait_recv()
        done = (own[n] + part_in[n].astype(jnp.float32)) / math.sqrt(4 * width)
        feat[b] = done.astype(jnp.bfloat16).reshape(2, n_ex, half)
        for k in (oc,) if n == 0 else (c, oc):
            t = b * 2 + k
            slot = 0 if n == 0 else (1 if k is c else 2)
            start(feat.at[b, k], feat_in.at[x], send_f.at[slot], recv_f.at[x], z, t)
    feat_in[x] = feat[xc, c]

    everyone = feat[...].reshape(4 * n_ex, half)
    for t in range(4):
        block = lax.dot_general(
            everyone, feat[t // 2, t % 2], (((1,), (1,)), ((), ())), preferred_element_type=jnp.float32
        ) / FEATS
        for row in range(4):
            gram[row * 4 + t] = block[row * n_ex:(row + 1) * n_ex].astype(jnp.bfloat16)
    for d in range(1, 16):
        t = (me + d) % 16
        start(gram.at[t], gram_in.at[me], send_k.at[d], recv_k.at[me], t // 4, t % 4)

    for d in range(4):
        t = (x + d) % 4
        if d:
            remote(feat_in.at[t], feat_in.at[t], send_f.at[0], recv_f.at[t], z, t).wait_recv()
        feats_ref[pl.ds(pl.multiple_of(t * half, half), half), :] = feat_in[t].T

    total = gram[me].astype(jnp.float32)
    for d in range(1, 16):
        t = (me + d) % 16
        remote(gram_in.at[t], gram_in.at[t], send_k.at[0], recv_k.at[t], t // 4, t % 4).wait_recv()
        total = total + gram_in[t].astype(jnp.float32)
    kern_ref[...] = total
    for copy in sends:
        copy.wait_send()


def fused(gradients, hash_salt, slab_offset):
    n_ex, width = gradients.shape
    half = FEATS // 16
    dma = pltpu.SemaphoreType.DMA
    return pl.pallas_call(
        fused_kernel,
        out_shape=(
            jax.ShapeDtypeStruct((FEATS // 4, n_ex), jnp.bfloat16),
            jax.ShapeDtypeStruct((n_ex, n_ex), jnp.float32),
        ),
        in_specs=[pl.BlockSpec(memory_space=pltpu.SMEM)] * 2 + [pl.BlockSpec(memory_space=pltpu.VMEM)],
        out_specs=(pl.BlockSpec(memory_space=pltpu.VMEM),) * 2,
        scratch_shapes=[
            pltpu.VMEM((2, 2, 2, n_ex, width), jnp.bfloat16),
            pltpu.VMEM((2, half, 2 * width), jnp.bfloat16),
            pltpu.VMEM((16, 2 * width), jnp.int32),
            pltpu.VMEM((2, 2 * n_ex, half), jnp.bfloat16),
            pltpu.VMEM((2, 2 * n_ex, half), jnp.bfloat16),
            pltpu.VMEM((2, 2 * n_ex, half), jnp.float32),
            pltpu.VMEM((2, 2, n_ex, half), jnp.bfloat16),
            pltpu.VMEM((4, n_ex, half), jnp.bfloat16),
            pltpu.VMEM((16, n_ex, n_ex), jnp.bfloat16),
            pltpu.VMEM((16, n_ex, n_ex), jnp.bfloat16),
            dma((7,)), dma((2, 2, 2)),
            dma((2,)), dma((2,)),
            dma((3,)), dma((4,)),
            dma((16,)), dma((16,)),
        ],
        compiler_params=pltpu.CompilerParams(
            collective_id=0, has_side_effects=True, vmem_limit_bytes=48 * 2**20
        ),
    )(hash_salt, slab_offset, gradients)


def solution(mesh):
    small = mesh.shape["coord"] == 4 and mesh.shape["ex"] == 4
    return jax.shard_map(
        fused if small else general,
        mesh=mesh,
        in_specs=(P(("groups", "ex"), "coord"), P("groups"), P("groups")),
        out_specs=(P("coord", ("groups", "ex")), P(("groups", "coord"), "ex")),
        check_vma=False,
    )
```

```python
import functools
import math

import jax
import jax.numpy as jnp
import numpy as np
from jax import lax
from jax.experimental import pallas as pl
from jax.experimental.pallas import tpu as pltpu
from jax.sharding import PartitionSpec as P

FEATS = 8192
LAST = int(np.array((1274126177 << 6) & 0xFFFFFFFF, np.uint32).astype(np.int32))


def sign_tile(coord_term, feat_term):
    m = coord_term ^ feat_term
    m = m ^ lax.shift_right_logical(m, jnp.int32(15))
    m = m * jnp.int32(73244475)
    m = m ^ lax.shift_right_logical(m, jnp.int32(13))
    p = m * jnp.int32(LAST)
    p = p ^ (p << 16)
    return jnp.where(p < 0, -1.0, 1.0).astype(jnp.bfloat16)


def project_kernel(sub, feat_rows, block, salt_ref, first_ref, place_ref, grads_ref, out_ref, signs, coord_term):
    coords = grads_ref.shape[1]
    step = pl.program_id(0)

    @pl.when(step == 0)
    def _():
        ids = first_ref[0] + lax.broadcasted_iota(jnp.int32, (16, coords), 1)
        coord_term[...] = (ids * 2654435) ^ salt_ref[0]

    @pl.loop(0, block // 16)
    def _(i):
        row = step * block + i * 16
        feat = (row // sub) * feat_rows + place_ref[0] * sub + row % sub
        feat_term = (feat + lax.broadcasted_iota(jnp.int32, (16, 128), 0)) * 97001
        for j in range(coords // 128):
            signs[pl.ds(pl.multiple_of(i * 16, 16), 16), pl.ds(j * 128, 128)] = sign_tile(
                coord_term[:, pl.ds(j * 128, 128)], feat_term
            )

    out_ref[...] = lax.dot_general(
        signs[...], grads_ref[...], (((1,), (1,)), ((), ())), preferred_element_type=jnp.float32
    ).astype(out_ref.dtype)


def project(gathered, salt, first, place, rows, sub, feat_rows):
    examples, coords = gathered.shape
    block = 512
    return pl.pallas_call(
        functools.partial(project_kernel, sub, feat_rows, block),
        grid=(rows // block,),
        out_shape=jax.ShapeDtypeStruct((rows, examples), jnp.bfloat16),
        in_specs=[pl.BlockSpec(memory_space=pltpu.SMEM)] * 3
        + [pl.BlockSpec((examples, coords), lambda i: (0, 0))],
        out_specs=pl.BlockSpec((block, examples), lambda i: (i, 0)),
        scratch_shapes=[
            pltpu.VMEM((block, coords), jnp.bfloat16),
            pltpu.VMEM((16, coords), jnp.int32),
        ],
        compiler_params=pltpu.CompilerParams(vmem_limit_bytes=40 * 2**20),
    )(salt, first, place, gathered)


def general(gradients, hash_salt, slab_offset):
    coord_local = gradients.shape[1]
    coord_parts = lax.axis_size("coord")
    ex_parts = lax.axis_size("ex")
    examples = gradients.shape[0] * ex_parts
    ex_local = gradients.shape[0]
    feat_rows = FEATS // coord_parts
    sub = feat_rows // ex_parts
    first = slab_offset + lax.axis_index("coord") * coord_local
    place = lax.axis_index("ex").reshape(1)
    gathered = lax.all_gather(gradients, "ex", axis=0, tiled=True)
    part = project(gathered, hash_salt, first, place, FEATS // ex_parts, sub, feat_rows)
    parts = lax.all_to_all(part.reshape(coord_parts, sub, examples), "coord", 0, 0)
    sums = jnp.sum(parts.astype(jnp.float32), axis=0)
    own = (sums / math.sqrt(coord_local * coord_parts)).astype(jnp.bfloat16)
    blocks = own.reshape(sub, ex_parts, ex_local).transpose(1, 0, 2)
    features = lax.all_to_all(blocks, "ex", 0, 0).reshape(feat_rows, ex_local)
    gram = lax.dot_general(own, own, (((0,), (0,)), ((), ())), preferred_element_type=jnp.float32) / FEATS
    gram = gram.astype(jnp.bfloat16).reshape(examples, ex_parts, ex_local).transpose(1, 0, 2)
    gram = jnp.sum(lax.all_to_all(gram, "ex", 0, 0).astype(jnp.float32), axis=0)
    gram = gram.astype(jnp.bfloat16).reshape(coord_parts, examples // coord_parts, ex_local)
    kernel = jnp.sum(lax.all_to_all(gram, "coord", 0, 0).astype(jnp.float32), axis=0)
    return features, kernel


def fused_kernel(
    salt_ref, offset_ref, grads_ref, feats_ref, kern_ref,
    grads, signs, coord_term, part, part_in, own, feat, feat_in, gram, gram_sib, gram_out, gram_in,
    local, send_g, recv_g, send_p, recv_p, send_f, recv_f, send_s, recv_s, send_k, recv_k,
):
    z, x = lax.axis_index("coord"), lax.axis_index("ex")
    xc, c = x // 2, x % 2
    zz = z % 2
    z_pair, z_far = z + 1 - 2 * zz, (z + 2) % 4
    oc, oz = 1 - c, 1 - zz
    ox = 1 - xc
    me = z * 4 + x
    n_ex, width = grads_ref.shape
    cut = n_ex // 2
    half = signs.shape[1]
    feat_rows = FEATS // 4
    sends = []

    def remote(src, dst, send, recv, zt, xt):
        return pltpu.make_async_remote_copy(
            src_ref=src, dst_ref=dst, send_sem=send, recv_sem=recv,
            device_id={"coord": zt, "ex": xt}, device_id_type=pl.DeviceIdType.MESH,
        )

    def start(*args):
        copy = remote(*args)
        copy.start()
        sends.append(copy)

    barrier = pltpu.get_barrier_semaphore()
    for d in range(1, 16):
        t = (me + d) % 16
        pl.semaphore_signal(
            barrier, inc=1, device_id={"coord": t // 4, "ex": t % 4}, device_id_type=pl.DeviceIdType.MESH
        )
    ids = offset_ref[0] + (z // 2) * (2 * width) + lax.broadcasted_iota(jnp.int32, (16, 2 * width), 1)
    coord_term[...] = (ids * 2654435) ^ salt_ref[0]
    pl.semaphore_wait(barrier, 15)

    copies = []
    for n, (zt, xt, cuts) in enumerate(((z_pair, x, (0, 1)), (z, ox * 2 + c, (1, 0)), (z, xc * 2 + oc, (0, 1)))):
        for k in cuts:
            start(
                grads_ref.at[pl.ds(k * cut, cut)], grads.at[zz, xc, k, c],
                send_g.at[2 * n + k], recv_g.at[zz, xc, k, c], zt, xt,
            )
    for k in range(2):
        copy = pltpu.make_async_copy(grads_ref.at[pl.ds(k * cut, cut)], grads.at[zz, xc, k, c], local.at[k])
        copy.start()
        copies.append(copy)

    def hash_rows(low, high):
        @pl.loop(low, high)
        def _(i):
            h = i // (half // 16)
            r = i % (half // 16)
            first = ((z + 2 * h) % 4) * feat_rows + x * half + r * 16
            feat_term = (first + lax.broadcasted_iota(jnp.int32, (16, 128), 0)) * 97001
            for j in range(2 * width // 128):
                signs[h, pl.ds(pl.multiple_of(r * 16, 16), 16), pl.ds(j * 128, 128)] = sign_tile(
                    coord_term[:, pl.ds(j * 128, 128)], feat_term
                )

    def arrived(a, b, k, core):
        slot = grads.at[a, b, k, core]
        remote(slot, slot, send_g.at[0], recv_g.at[a, b, k, core], z_pair, x).wait_recv()

    def pass_on(a, b, k, n, zt, xt):
        slot = grads.at[a, b, k, c]
        start(slot, slot, send_g.at[n], recv_g.at[a, b, k, c], zt, xt)

    def forward(a, b, k, n):
        pass_on(a, b, k, n, z, xc * 2 + oc)

    def sums(b, k, h):
        total = None
        for a in range(2):
            one = lax.dot_general(
                grads[a, b, k].reshape(n_ex, width), signs[h, :, pl.ds(a * width, width)],
                (((1,), (1,)), ((), ())), preferred_element_type=jnp.float32,
            )
            total = one if total is None else total + one
        return total

    def exchange(n):
        return remote(part.at[n], part_in.at[n], send_p.at[n], recv_p.at[n], z_far, x)

    def give(n, b, k):
        arrived(zz, b, k, oc)
        arrived(oz, b, k, oc)
        part[n] = sums(b, k, 1).astype(jnp.bfloat16)
        copy = exchange(n)
        copy.start()
        sends.append(copy)

    steps = half // 16
    hash_rows(steps, 2 * steps)
    for copy in copies:
        copy.wait()
    arrived(oz, xc, 0, c)
    pass_on(oz, xc, 0, 6, z, ox * 2 + c)
    forward(oz, xc, 0, 8)
    arrived(zz, ox, 1, c)
    pass_on(zz, ox, 1, 7, z_pair, x)
    forward(zz, ox, 1, 9)
    give(0, xc, 0)
    hash_rows(0, steps // 2)
    arrived(oz, xc, 1, c)
    forward(oz, xc, 1, 10)
    give(1, xc, 1)
    arrived(zz, ox, 0, c)
    forward(zz, ox, 0, 11)
    hash_rows(steps // 2, steps)
    arrived(oz, ox, 0, c)
    forward(oz, ox, 0, 12)
    give(2, ox, 0)
    arrived(oz, ox, 1, c)
    forward(oz, ox, 1, 13)
    give(3, ox, 1)
    chunks = ((xc, 0), (xc, 1), (ox, 0), (ox, 1))
    for n, (b, k) in enumerate(chunks):
        own[n] = sums(b, k, 0)

    for n, (b, k) in enumerate(chunks):
        exchange(n).wait_recv()
        done = (own[n] + part_in[n].astype(jnp.float32)) / math.sqrt(4 * width)
        feat[b, :, pl.ds(k * cut, cut)] = done.astype(jnp.bfloat16).reshape(2, cut, half)
        if n == 1:
            start(feat.at[xc, oc], feat_in.at[x], send_f.at[0], recv_f.at[x], z, xc * 2 + oc)
        if n == 3:
            start(feat.at[ox, c], feat_in.at[x], send_f.at[1], recv_f.at[x], z, ox * 2 + c)
            start(feat.at[ox, oc], feat_in.at[x], send_f.at[2], recv_f.at[x], z, ox * 2 + oc)

    everyone = feat[...].reshape(4 * n_ex, half)

    def blocks(core):
        for b in range(2):
            block = lax.dot_general(
                everyone, feat[b, core], (((1,), (1,)), ((), ())), preferred_element_type=jnp.float32
            ) / FEATS
            for row in range(4):
                gram[core, row * 2 + b] = block[row * n_ex:(row + 1) * n_ex].astype(jnp.bfloat16)

    chip = z * 2 + xc
    blocks(oc)
    sibling = remote(gram.at[oc], gram_sib, send_s, recv_s, z, xc * 2 + oc)
    sibling.start()
    sends.append(sibling)
    blocks(c)
    feat_in[x] = feat[xc, c]
    sibling.wait_recv()
    gram_out[...] = (gram[c].astype(jnp.float32) + gram_sib[...].astype(jnp.float32)).astype(jnp.bfloat16)
    for d in range(1, 8):
        t = (chip + d) % 8
        start(
            gram_out.at[t], gram_in.at[chip], send_k.at[d], recv_k.at[chip], t // 2, (t % 2) * 2 + c
        )

    for d in range(4):
        t = (x + d) % 4
        if d:
            remote(feat_in.at[t], feat_in.at[t], send_f.at[0], recv_f.at[t], z, t).wait_recv()
        feats_ref[:, pl.ds(pl.multiple_of(t * half, half), half)] = feat_in[t]

    total = gram[c, chip].astype(jnp.float32) + gram_sib[chip].astype(jnp.float32)
    for d in range(1, 8):
        t = (chip + d) % 8
        remote(
            gram_in.at[t], gram_in.at[t], send_k.at[0], recv_k.at[t], t // 2, (t % 2) * 2 + c
        ).wait_recv()
        total = total + gram_in[t].astype(jnp.float32)
    kern_ref[...] = total
    for copy in sends:
        copy.wait_send()


def fused(gradients, hash_salt, slab_offset):
    n_ex, width = gradients.shape
    half = FEATS // 16
    dma = pltpu.SemaphoreType.DMA
    flipped, kernel = pl.pallas_call(
        fused_kernel,
        out_shape=(
            jax.ShapeDtypeStruct((n_ex, FEATS // 4), jnp.bfloat16),
            jax.ShapeDtypeStruct((n_ex, n_ex), jnp.float32),
        ),
        in_specs=[pl.BlockSpec(memory_space=pltpu.SMEM)] * 2 + [pl.BlockSpec(memory_space=pltpu.HBM)],
        out_specs=(pl.BlockSpec(memory_space=pltpu.VMEM),) * 2,
        scratch_shapes=[
            pltpu.VMEM((2, 2, 2, 2, n_ex // 2, width), jnp.bfloat16),
            pltpu.VMEM((2, half, 2 * width), jnp.bfloat16),
            pltpu.VMEM((16, 2 * width), jnp.int32),
            pltpu.VMEM((4, n_ex, half), jnp.bfloat16),
            pltpu.VMEM((4, n_ex, half), jnp.bfloat16),
            pltpu.VMEM((4, n_ex, half), jnp.float32),
            pltpu.VMEM((2, 2, n_ex, half), jnp.bfloat16),
            pltpu.VMEM((4, n_ex, half), jnp.bfloat16),
            pltpu.VMEM((2, 8, n_ex, n_ex), jnp.bfloat16),
            pltpu.VMEM((8, n_ex, n_ex), jnp.bfloat16),
            pltpu.VMEM((8, n_ex, n_ex), jnp.bfloat16),
            pltpu.VMEM((8, n_ex, n_ex), jnp.bfloat16),
            dma((2,)), dma((14,)), dma((2, 2, 2, 2)),
            dma((4,)), dma((4,)),
            dma((3,)), dma((4,)),
            dma, dma,
            dma((8,)), dma((8,)),
        ],
        compiler_params=pltpu.CompilerParams(
            collective_id=0, has_side_effects=True, vmem_limit_bytes=48 * 2**20
        ),
    )(hash_salt, slab_offset, gradients)
    return flipped.T, kernel


def solution(mesh):
    small = mesh.shape["coord"] == 4 and mesh.shape["ex"] == 4
    return jax.shard_map(
        fused if small else general,
        mesh=mesh,
        in_specs=(P(("groups", "ex"), "coord"), P("groups"), P("groups")),
        out_specs=(P("coord", ("groups", "ex")), P(("groups", "coord"), "ex")),
        check_vma=False,
    )
```

```python
import functools
import math

import jax
import jax.numpy as jnp
import numpy as np
from jax import lax
from jax.experimental import pallas as pl
from jax.experimental.pallas import tpu as pltpu
from jax.sharding import PartitionSpec as P

FEATS = 8192
LAST = int(np.array((1274126177 << 6) & 0xFFFFFFFF, np.uint32).astype(np.int32))


def sign_tile(coord_term, feat_term):
    m = coord_term ^ feat_term
    m = m ^ lax.shift_right_logical(m, jnp.int32(15))
    m = m * jnp.int32(73244475)
    m = m ^ lax.shift_right_logical(m, jnp.int32(13))
    p = m * jnp.int32(LAST)
    p = p ^ (p << 16)
    return jnp.where(p < 0, -1.0, 1.0).astype(jnp.bfloat16)


def project_kernel(sub, feat_rows, block, salt_ref, first_ref, place_ref, grads_ref, out_ref, signs, coord_term):
    coords = grads_ref.shape[1]
    step = pl.program_id(0)

    @pl.when(step == 0)
    def _():
        ids = first_ref[0] + lax.broadcasted_iota(jnp.int32, (16, coords), 1)
        coord_term[...] = (ids * 2654435) ^ salt_ref[0]

    @pl.loop(0, block // 16)
    def _(i):
        row = step * block + i * 16
        feat = (row // sub) * feat_rows + place_ref[0] * sub + row % sub
        feat_term = (feat + lax.broadcasted_iota(jnp.int32, (16, 128), 0)) * 97001
        for j in range(coords // 128):
            signs[pl.ds(pl.multiple_of(i * 16, 16), 16), pl.ds(j * 128, 128)] = sign_tile(
                coord_term[:, pl.ds(j * 128, 128)], feat_term
            )

    out_ref[...] = lax.dot_general(
        signs[...], grads_ref[...], (((1,), (1,)), ((), ())), preferred_element_type=jnp.float32
    ).astype(out_ref.dtype)


def project(gathered, salt, first, place, rows, sub, feat_rows):
    examples, coords = gathered.shape
    block = 512
    return pl.pallas_call(
        functools.partial(project_kernel, sub, feat_rows, block),
        grid=(rows // block,),
        out_shape=jax.ShapeDtypeStruct((rows, examples), jnp.bfloat16),
        in_specs=[pl.BlockSpec(memory_space=pltpu.SMEM)] * 3
        + [pl.BlockSpec((examples, coords), lambda i: (0, 0))],
        out_specs=pl.BlockSpec((block, examples), lambda i: (i, 0)),
        scratch_shapes=[
            pltpu.VMEM((block, coords), jnp.bfloat16),
            pltpu.VMEM((16, coords), jnp.int32),
        ],
        compiler_params=pltpu.CompilerParams(vmem_limit_bytes=40 * 2**20),
    )(salt, first, place, gathered)


def general(gradients, hash_salt, slab_offset):
    coord_local = gradients.shape[1]
    coord_parts = lax.axis_size("coord")
    ex_parts = lax.axis_size("ex")
    examples = gradients.shape[0] * ex_parts
    ex_local = gradients.shape[0]
    feat_rows = FEATS // coord_parts
    sub = feat_rows // ex_parts
    first = slab_offset + lax.axis_index("coord") * coord_local
    place = lax.axis_index("ex").reshape(1)
    gathered = lax.all_gather(gradients, "ex", axis=0, tiled=True)
    part = project(gathered, hash_salt, first, place, FEATS // ex_parts, sub, feat_rows)
    parts = lax.all_to_all(part.reshape(coord_parts, sub, examples), "coord", 0, 0)
    sums = jnp.sum(parts.astype(jnp.float32), axis=0)
    own = (sums / math.sqrt(coord_local * coord_parts)).astype(jnp.bfloat16)
    blocks = own.reshape(sub, ex_parts, ex_local).transpose(1, 0, 2)
    features = lax.all_to_all(blocks, "ex", 0, 0).reshape(feat_rows, ex_local)
    gram = lax.dot_general(own, own, (((0,), (0,)), ((), ())), preferred_element_type=jnp.float32) / FEATS
    gram = gram.astype(jnp.bfloat16).reshape(examples, ex_parts, ex_local).transpose(1, 0, 2)
    gram = jnp.sum(lax.all_to_all(gram, "ex", 0, 0).astype(jnp.float32), axis=0)
    gram = gram.astype(jnp.bfloat16).reshape(coord_parts, examples // coord_parts, ex_local)
    kernel = jnp.sum(lax.all_to_all(gram, "coord", 0, 0).astype(jnp.float32), axis=0)
    return features, kernel


def fused_kernel(
    salt_ref, offset_ref, grads_ref, feats_ref, kern_ref,
    grads, signs, coord_term, part, part_in, own, feat, feat_in, gram, gram_sib, gram_out, gram_in,
    local, send_g, recv_g, send_p, recv_p, send_f, recv_f, send_s, recv_s, send_k, recv_k,
):
    z, x = lax.axis_index("coord"), lax.axis_index("ex")
    xc, c = x // 2, x % 2
    zz = z % 2
    z_pair, z_far = z + 1 - 2 * zz, (z + 2) % 4
    oc, oz = 1 - c, 1 - zz
    ox = 1 - xc
    me = z * 4 + x
    n_ex, width = grads_ref.shape
    cut = n_ex // 2
    half = signs.shape[1]
    feat_rows = FEATS // 4
    sends = []

    def remote(src, dst, send, recv, zt, xt):
        return pltpu.make_async_remote_copy(
            src_ref=src, dst_ref=dst, send_sem=send, recv_sem=recv,
            device_id={"coord": zt, "ex": xt}, device_id_type=pl.DeviceIdType.MESH,
        )

    def start(*args):
        copy = remote(*args)
        copy.start()
        sends.append(copy)

    barrier = pltpu.get_barrier_semaphore()
    for d in range(1, 16):
        t = (me + d) % 16
        pl.semaphore_signal(
            barrier, inc=1, device_id={"coord": t // 4, "ex": t % 4}, device_id_type=pl.DeviceIdType.MESH
        )
    ids = offset_ref[0] + (z // 2) * (2 * width) + lax.broadcasted_iota(jnp.int32, (16, 2 * width), 1)
    coord_term[...] = (ids * 2654435) ^ salt_ref[0]
    pl.semaphore_wait(barrier, 15)

    copies = []
    for n, (zt, xt, cuts) in enumerate(((z_pair, x, (0, 1)), (z, ox * 2 + c, (0, 1)), (z, xc * 2 + oc, (0, 1)))):
        for k in cuts:
            start(
                grads_ref.at[pl.ds(k * cut, cut)], grads.at[zz, xc, k, c],
                send_g.at[2 * n + k], recv_g.at[zz, xc, k, c], zt, xt,
            )
    for k in range(2):
        copy = pltpu.make_async_copy(grads_ref.at[pl.ds(k * cut, cut)], grads.at[zz, xc, k, c], local.at[k])
        copy.start()
        copies.append(copy)

    def hash_rows(low, high):
        @pl.loop(low, high)
        def _(i):
            h = i // (half // 16)
            r = i % (half // 16)
            first = ((z + 2 * h) % 4) * feat_rows + x * half + r * 16
            feat_term = (first + lax.broadcasted_iota(jnp.int32, (16, 128), 0)) * 97001
            for j in range(2 * width // 128):
                signs[h, pl.ds(pl.multiple_of(r * 16, 16), 16), pl.ds(j * 128, 128)] = sign_tile(
                    coord_term[:, pl.ds(j * 128, 128)], feat_term
                )

    def arrived(a, b, k, core):
        slot = grads.at[a, b, k, core]
        remote(slot, slot, send_g.at[0], recv_g.at[a, b, k, core], z_pair, x).wait_recv()

    def pass_on(a, b, k, n, zt, xt):
        slot = grads.at[a, b, k, c]
        start(slot, slot, send_g.at[n], recv_g.at[a, b, k, c], zt, xt)

    def forward(a, b, k, n):
        pass_on(a, b, k, n, z, xc * 2 + oc)

    def sums(b, k, h):
        total = None
        for a in range(2):
            one = lax.dot_general(
                grads[a, b, k].reshape(n_ex, width), signs[h, :, pl.ds(a * width, width)],
                (((1,), (1,)), ((), ())), preferred_element_type=jnp.float32,
            )
            total = one if total is None else total + one
        return total

    def exchange(n):
        return remote(part.at[n], part_in.at[n], send_p.at[n], recv_p.at[n], z_far, x)

    def give(n, b, k):
        arrived(zz, b, k, oc)
        arrived(oz, b, k, oc)
        part[n] = sums(b, k, 1).astype(jnp.bfloat16)
        copy = exchange(n)
        copy.start()
        sends.append(copy)

    steps = half // 16
    hash_rows(steps, 2 * steps)
    for copy in copies:
        copy.wait()
    arrived(oz, xc, 0, c)
    pass_on(oz, xc, 0, 6, z, ox * 2 + c)
    forward(oz, xc, 0, 8)
    give(0, xc, 0)
    hash_rows(0, steps // 2)
    arrived(oz, xc, 1, c)
    pass_on(oz, xc, 1, 7, z, ox * 2 + c)
    forward(oz, xc, 1, 10)
    give(1, xc, 1)
    arrived(zz, ox, 0, c)
    forward(zz, ox, 0, 11)
    arrived(zz, ox, 1, c)
    forward(zz, ox, 1, 9)
    hash_rows(steps // 2, steps)
    arrived(oz, ox, 0, c)
    forward(oz, ox, 0, 12)
    give(2, ox, 0)
    arrived(oz, ox, 1, c)
    forward(oz, ox, 1, 13)
    give(3, ox, 1)
    chunks = ((xc, 0), (xc, 1), (ox, 0), (ox, 1))
    for n, (b, k) in enumerate(chunks):
        own[n] = sums(b, k, 0)

    for n, (b, k) in enumerate(chunks):
        exchange(n).wait_recv()
        done = (own[n] + part_in[n].astype(jnp.float32)) / math.sqrt(4 * width)
        feat[b, :, pl.ds(k * cut, cut)] = done.astype(jnp.bfloat16).reshape(2, cut, half)
        if n == 1:
            start(feat.at[xc, oc], feat_in.at[x], send_f.at[0], recv_f.at[x], z, xc * 2 + oc)
        if n == 3:
            start(feat.at[ox, c], feat_in.at[x], send_f.at[1], recv_f.at[x], z, ox * 2 + c)
            start(feat.at[ox, oc], feat_in.at[x], send_f.at[2], recv_f.at[x], z, ox * 2 + oc)

    everyone = feat[...].reshape(4 * n_ex, half)

    def blocks(core):
        for b in range(2):
            block = lax.dot_general(
                everyone, feat[b, core], (((1,), (1,)), ((), ())), preferred_element_type=jnp.float32
            ) / FEATS
            for row in range(4):
                gram[core, row * 2 + b] = block[row * n_ex:(row + 1) * n_ex].astype(jnp.bfloat16)

    chip = z * 2 + xc
    blocks(oc)
    sibling = remote(gram.at[oc], gram_sib, send_s, recv_s, z, xc * 2 + oc)
    sibling.start()
    sends.append(sibling)
    blocks(c)
    feat_in[x] = feat[xc, c]
    sibling.wait_recv()
    gram_out[...] = (gram[c].astype(jnp.float32) + gram_sib[...].astype(jnp.float32)).astype(jnp.bfloat16)
    for d in range(1, 8):
        t = (chip + d) % 8
        start(
            gram_out.at[t], gram_in.at[chip], send_k.at[d], recv_k.at[chip], t // 2, (t % 2) * 2 + c
        )

    for d in range(4):
        t = (x + d) % 4
        if d:
            remote(feat_in.at[t], feat_in.at[t], send_f.at[0], recv_f.at[t], z, t).wait_recv()
        feats_ref[:, pl.ds(pl.multiple_of(t * half, half), half)] = feat_in[t]

    total = gram[c, chip].astype(jnp.float32) + gram_sib[chip].astype(jnp.float32)
    for d in range(1, 8):
        t = (chip + d) % 8
        remote(
            gram_in.at[t], gram_in.at[t], send_k.at[0], recv_k.at[t], t // 2, (t % 2) * 2 + c
        ).wait_recv()
        total = total + gram_in[t].astype(jnp.float32)
    kern_ref[...] = total
    for copy in sends:
        copy.wait_send()


def fused(gradients, hash_salt, slab_offset):
    n_ex, width = gradients.shape
    half = FEATS // 16
    dma = pltpu.SemaphoreType.DMA
    flipped, kernel = pl.pallas_call(
        fused_kernel,
        out_shape=(
            jax.ShapeDtypeStruct((n_ex, FEATS // 4), jnp.bfloat16),
            jax.ShapeDtypeStruct((n_ex, n_ex), jnp.float32),
        ),
        in_specs=[pl.BlockSpec(memory_space=pltpu.SMEM)] * 2 + [pl.BlockSpec(memory_space=pltpu.HBM)],
        out_specs=(pl.BlockSpec(memory_space=pltpu.VMEM),) * 2,
        scratch_shapes=[
            pltpu.VMEM((2, 2, 2, 2, n_ex // 2, width), jnp.bfloat16),
            pltpu.VMEM((2, half, 2 * width), jnp.bfloat16),
            pltpu.VMEM((16, 2 * width), jnp.int32),
            pltpu.VMEM((4, n_ex, half), jnp.bfloat16),
            pltpu.VMEM((4, n_ex, half), jnp.bfloat16),
            pltpu.VMEM((4, n_ex, half), jnp.float32),
            pltpu.VMEM((2, 2, n_ex, half), jnp.bfloat16),
            pltpu.VMEM((4, n_ex, half), jnp.bfloat16),
            pltpu.VMEM((2, 8, n_ex, n_ex), jnp.bfloat16),
            pltpu.VMEM((8, n_ex, n_ex), jnp.bfloat16),
            pltpu.VMEM((8, n_ex, n_ex), jnp.bfloat16),
            pltpu.VMEM((8, n_ex, n_ex), jnp.bfloat16),
            dma((2,)), dma((14,)), dma((2, 2, 2, 2)),
            dma((4,)), dma((4,)),
            dma((3,)), dma((4,)),
            dma, dma,
            dma((8,)), dma((8,)),
        ],
        compiler_params=pltpu.CompilerParams(
            collective_id=0, has_side_effects=True, vmem_limit_bytes=48 * 2**20
        ),
    )(hash_salt, slab_offset, gradients)
    return flipped.T, kernel


def solution(mesh):
    small = mesh.shape["coord"] == 4 and mesh.shape["ex"] == 4
    return jax.shard_map(
        fused if small else general,
        mesh=mesh,
        in_specs=(P(("groups", "ex"), "coord"), P("groups"), P("groups")),
        out_specs=(P("coord", ("groups", "ex")), P(("groups", "coord"), "ex")),
        check_vma=False,
    )
```

```python
import functools
import math

import jax
import jax.numpy as jnp
import numpy as np
from jax import lax
from jax.experimental import pallas as pl
from jax.experimental.pallas import tpu as pltpu
from jax.sharding import PartitionSpec as P

FEATS = 8192
LAST = int(np.array((1274126177 << 6) & 0xFFFFFFFF, np.uint32).astype(np.int32))


def sign_tile(coord_term, feat_term):
    m = coord_term ^ feat_term
    m = m ^ lax.shift_right_logical(m, jnp.int32(15))
    m = m * jnp.int32(73244475)
    m = m ^ lax.shift_right_logical(m, jnp.int32(13))
    p = m * jnp.int32(LAST)
    p = p ^ (p << 16)
    return jnp.where(p < 0, -1.0, 1.0).astype(jnp.bfloat16)


def project_kernel(sub, feat_rows, block, salt_ref, first_ref, place_ref, grads_ref, out_ref, signs, coord_term):
    coords = grads_ref.shape[1]
    step = pl.program_id(0)

    @pl.when(step == 0)
    def _():
        ids = first_ref[0] + lax.broadcasted_iota(jnp.int32, (16, coords), 1)
        coord_term[...] = (ids * 2654435) ^ salt_ref[0]

    @pl.loop(0, block // 16)
    def _(i):
        row = step * block + i * 16
        feat = (row // sub) * feat_rows + place_ref[0] * sub + row % sub
        feat_term = (feat + lax.broadcasted_iota(jnp.int32, (16, 128), 0)) * 97001
        for j in range(coords // 128):
            signs[pl.ds(pl.multiple_of(i * 16, 16), 16), pl.ds(j * 128, 128)] = sign_tile(
                coord_term[:, pl.ds(j * 128, 128)], feat_term
            )

    out_ref[...] = lax.dot_general(
        signs[...], grads_ref[...], (((1,), (1,)), ((), ())), preferred_element_type=jnp.float32
    ).astype(out_ref.dtype)


def project(gathered, salt, first, place, rows, sub, feat_rows):
    examples, coords = gathered.shape
    block = 512
    return pl.pallas_call(
        functools.partial(project_kernel, sub, feat_rows, block),
        grid=(rows // block,),
        out_shape=jax.ShapeDtypeStruct((rows, examples), jnp.bfloat16),
        in_specs=[pl.BlockSpec(memory_space=pltpu.SMEM)] * 3
        + [pl.BlockSpec((examples, coords), lambda i: (0, 0))],
        out_specs=pl.BlockSpec((block, examples), lambda i: (i, 0)),
        scratch_shapes=[
            pltpu.VMEM((block, coords), jnp.bfloat16),
            pltpu.VMEM((16, coords), jnp.int32),
        ],
        compiler_params=pltpu.CompilerParams(vmem_limit_bytes=40 * 2**20),
    )(salt, first, place, gathered)


def general(gradients, hash_salt, slab_offset):
    coord_local = gradients.shape[1]
    coord_parts = lax.axis_size("coord")
    ex_parts = lax.axis_size("ex")
    examples = gradients.shape[0] * ex_parts
    ex_local = gradients.shape[0]
    feat_rows = FEATS // coord_parts
    sub = feat_rows // ex_parts
    first = slab_offset + lax.axis_index("coord") * coord_local
    place = lax.axis_index("ex").reshape(1)
    gathered = lax.all_gather(gradients, "ex", axis=0, tiled=True)
    part = project(gathered, hash_salt, first, place, FEATS // ex_parts, sub, feat_rows)
    parts = lax.all_to_all(part.reshape(coord_parts, sub, examples), "coord", 0, 0)
    sums = jnp.sum(parts.astype(jnp.float32), axis=0)
    own = (sums / math.sqrt(coord_local * coord_parts)).astype(jnp.bfloat16)
    blocks = own.reshape(sub, ex_parts, ex_local).transpose(1, 0, 2)
    features = lax.all_to_all(blocks, "ex", 0, 0).reshape(feat_rows, ex_local)
    gram = lax.dot_general(own, own, (((0,), (0,)), ((), ())), preferred_element_type=jnp.float32) / FEATS
    gram = gram.astype(jnp.bfloat16).reshape(examples, ex_parts, ex_local).transpose(1, 0, 2)
    gram = jnp.sum(lax.all_to_all(gram, "ex", 0, 0).astype(jnp.float32), axis=0)
    gram = gram.astype(jnp.bfloat16).reshape(coord_parts, examples // coord_parts, ex_local)
    kernel = jnp.sum(lax.all_to_all(gram, "coord", 0, 0).astype(jnp.float32), axis=0)
    return features, kernel


def fused_kernel(
    salt_ref, offset_ref, grads_ref, feats_ref, kern_ref,
    grads, signs, coord_term, part, part_in, own, feat, feat_in, gram, gram_sib, gram_out, gram_in,
    local, send_g, recv_g, send_p, recv_p, send_f, recv_f, send_s, recv_s, send_k, recv_k,
):
    z, x = lax.axis_index("coord"), lax.axis_index("ex")
    xc, c = x // 2, x % 2
    zz = z % 2
    z_pair, z_far = z + 1 - 2 * zz, (z + 2) % 4
    oc, oz = 1 - c, 1 - zz
    ox = 1 - xc
    n_ex, width = grads_ref.shape
    cut = n_ex // 2
    half = signs.shape[1]
    feat_rows = FEATS // 4
    sends = []

    def remote(src, dst, send, recv, zt, xt):
        return pltpu.make_async_remote_copy(
            src_ref=src, dst_ref=dst, send_sem=send, recv_sem=recv,
            device_id={"coord": zt, "ex": xt}, device_id_type=pl.DeviceIdType.MESH,
        )

    def start(*args):
        copy = remote(*args)
        copy.start()
        sends.append(copy)

    barrier = pltpu.get_barrier_semaphore()
    chip = z * 2 + xc
    greeted = [(z, xc * 2 + oc), (z, ox * 2 + oc)]
    for d in range(1, 8):
        t = (chip + d) % 8
        greeted.append((t // 2, (t % 2) * 2 + c))
    for zt, xt in greeted:
        pl.semaphore_signal(
            barrier, inc=1, device_id={"coord": zt, "ex": xt}, device_id_type=pl.DeviceIdType.MESH
        )
    ids = offset_ref[0] + (z // 2) * (2 * width) + lax.broadcasted_iota(jnp.int32, (16, 2 * width), 1)
    coord_term[...] = (ids * 2654435) ^ salt_ref[0]
    pl.semaphore_wait(barrier, 9)

    copies = []
    for n, (zt, xt, cuts) in enumerate(((z_pair, x, (0, 1)), (z, ox * 2 + c, (0, 1)), (z, xc * 2 + oc, (0, 1)))):
        for k in cuts:
            start(
                grads_ref.at[pl.ds(k * cut, cut)], grads.at[zz, xc, k, c],
                send_g.at[2 * n + k], recv_g.at[zz, xc, k, c], zt, xt,
            )
    for k in range(2):
        copy = pltpu.make_async_copy(grads_ref.at[pl.ds(k * cut, cut)], grads.at[zz, xc, k, c], local.at[k])
        copy.start()
        copies.append(copy)

    def hash_rows(low, high):
        @pl.loop(low, high)
        def _(i):
            h = i // (half // 16)
            r = i % (half // 16)
            first = ((z + 2 * h) % 4) * feat_rows + x * half + r * 16
            feat_term = (first + lax.broadcasted_iota(jnp.int32, (16, 128), 0)) * 97001
            for j in range(2 * width // 128):
                signs[h, pl.ds(pl.multiple_of(r * 16, 16), 16), pl.ds(j * 128, 128)] = sign_tile(
                    coord_term[:, pl.ds(j * 128, 128)], feat_term
                )

    def arrived(a, b, k, core):
        slot = grads.at[a, b, k, core]
        remote(slot, slot, send_g.at[0], recv_g.at[a, b, k, core], z_pair, x).wait_recv()

    def pass_on(a, b, k, n, zt, xt):
        slot = grads.at[a, b, k, c]
        start(slot, slot, send_g.at[n], recv_g.at[a, b, k, c], zt, xt)

    def forward(a, b, k, n):
        pass_on(a, b, k, n, z, xc * 2 + oc)

    def sums(b, k, h):
        total = None
        for a in range(2):
            one = lax.dot_general(
                grads[a, b, k].reshape(n_ex, width), signs[h, :, pl.ds(a * width, width)],
                (((1,), (1,)), ((), ())), preferred_element_type=jnp.float32,
            )
            total = one if total is None else total + one
        return total

    def exchange(n):
        return remote(part.at[n], part_in.at[n], send_p.at[n], recv_p.at[n], z_far, x)

    def give(n, b, k):
        arrived(zz, b, k, oc)
        arrived(oz, b, k, oc)
        part[n] = sums(b, k, 1).astype(jnp.bfloat16)
        copy = exchange(n)
        copy.start()
        sends.append(copy)

    steps = half // 16
    hash_rows(steps, 2 * steps)
    for copy in copies:
        copy.wait()
    arrived(oz, xc, 0, c)
    pass_on(oz, xc, 0, 6, z, ox * 2 + c)
    forward(oz, xc, 0, 8)
    give(0, xc, 0)
    hash_rows(0, steps // 2)
    arrived(oz, xc, 1, c)
    pass_on(oz, xc, 1, 7, z, ox * 2 + c)
    forward(oz, xc, 1, 10)
    give(1, xc, 1)
    arrived(zz, ox, 0, c)
    forward(zz, ox, 0, 11)
    arrived(zz, ox, 1, c)
    forward(zz, ox, 1, 9)
    hash_rows(steps // 2, steps)
    own[0] = sums(xc, 0, 0)
    own[1] = sums(xc, 1, 0)
    arrived(oz, ox, 0, c)
    forward(oz, ox, 0, 12)
    give(2, ox, 0)
    own[2] = sums(ox, 0, 0)
    arrived(oz, ox, 1, c)
    forward(oz, ox, 1, 13)
    give(3, ox, 1)
    chunks = ((xc, 0), (xc, 1), (ox, 0), (ox, 1))
    own[3] = sums(ox, 1, 0)

    for n, (b, k) in enumerate(chunks):
        exchange(n).wait_recv()
        done = (own[n] + part_in[n].astype(jnp.float32)) / math.sqrt(4 * width)
        feat[b, :, pl.ds(k * cut, cut)] = done.astype(jnp.bfloat16).reshape(2, cut, half)
        rows = pl.ds(k * cut, cut)
        into = feat_in.at[x, rows]
        if n < 2:
            start(feat.at[xc, oc, rows], into, send_f.at[0, k], recv_f.at[x, k], z, xc * 2 + oc)
        else:
            start(feat.at[ox, c, rows], into, send_f.at[1, k], recv_f.at[x, k], z, ox * 2 + c)
            start(feat.at[ox, oc, rows], into, send_f.at[2, k], recv_f.at[x, k], z, ox * 2 + oc)

    everyone = feat[...].reshape(4 * n_ex, half)

    def blocks(core):
        for b in range(2):
            block = lax.dot_general(
                everyone, feat[b, core], (((1,), (1,)), ((), ())), preferred_element_type=jnp.float32
            ) / FEATS
            for row in range(4):
                gram[core, row * 2 + b] = block[row * n_ex:(row + 1) * n_ex].astype(jnp.bfloat16)

    blocks(oc)
    sibling = remote(gram.at[oc], gram_sib, send_s, recv_s, z, xc * 2 + oc)
    sibling.start()
    sends.append(sibling)
    blocks(c)
    feat_in[x] = feat[xc, c]
    sibling.wait_recv()
    gram_out[...] = (gram[c].astype(jnp.float32) + gram_sib[...].astype(jnp.float32)).astype(jnp.bfloat16)
    for d in range(1, 8):
        t = (chip + d) % 8
        start(
            gram_out.at[t], gram_in.at[chip], send_k.at[d], recv_k.at[chip], t // 2, (t % 2) * 2 + c
        )

    for d in range(4):
        t = (x + d) % 4
        if d:
            for k in range(2):
                slot = feat_in.at[t, pl.ds(k * cut, cut)]
                remote(slot, slot, send_f.at[0, k], recv_f.at[t, k], z, t).wait_recv()
        feats_ref[:, pl.ds(pl.multiple_of(t * half, half), half)] = feat_in[t]

    total = gram[c, chip].astype(jnp.float32) + gram_sib[chip].astype(jnp.float32)
    for d in range(1, 8):
        t = (chip + d) % 8
        remote(
            gram_in.at[t], gram_in.at[t], send_k.at[0], recv_k.at[t], t // 2, (t % 2) * 2 + c
        ).wait_recv()
        total = total + gram_in[t].astype(jnp.float32)
    kern_ref[...] = total
    for copy in sends:
        copy.wait_send()


def fused(gradients, hash_salt, slab_offset):
    n_ex, width = gradients.shape
    half = FEATS // 16
    dma = pltpu.SemaphoreType.DMA
    flipped, kernel = pl.pallas_call(
        fused_kernel,
        out_shape=(
            jax.ShapeDtypeStruct((n_ex, FEATS // 4), jnp.bfloat16),
            jax.ShapeDtypeStruct((n_ex, n_ex), jnp.float32),
        ),
        in_specs=[pl.BlockSpec(memory_space=pltpu.SMEM)] * 2 + [pl.BlockSpec(memory_space=pltpu.HBM)],
        out_specs=(pl.BlockSpec(memory_space=pltpu.VMEM),) * 2,
        scratch_shapes=[
            pltpu.VMEM((2, 2, 2, 2, n_ex // 2, width), jnp.bfloat16),
            pltpu.VMEM((2, half, 2 * width), jnp.bfloat16),
            pltpu.VMEM((16, 2 * width), jnp.int32),
            pltpu.VMEM((4, n_ex, half), jnp.bfloat16),
            pltpu.VMEM((4, n_ex, half), jnp.bfloat16),
            pltpu.VMEM((4, n_ex, half), jnp.float32),
            pltpu.VMEM((2, 2, n_ex, half), jnp.bfloat16),
            pltpu.VMEM((4, n_ex, half), jnp.bfloat16),
            pltpu.VMEM((2, 8, n_ex, n_ex), jnp.bfloat16),
            pltpu.VMEM((8, n_ex, n_ex), jnp.bfloat16),
            pltpu.VMEM((8, n_ex, n_ex), jnp.bfloat16),
            pltpu.VMEM((8, n_ex, n_ex), jnp.bfloat16),
            dma((2,)), dma((14,)), dma((2, 2, 2, 2)),
            dma((4,)), dma((4,)),
            dma((3, 2)), dma((4, 2)),
            dma, dma,
            dma((8,)), dma((8,)),
        ],
        compiler_params=pltpu.CompilerParams(
            collective_id=0, has_side_effects=True, vmem_limit_bytes=48 * 2**20
        ),
    )(hash_salt, slab_offset, gradients)
    return flipped.T, kernel


def solution(mesh):
    small = mesh.shape["coord"] == 4 and mesh.shape["ex"] == 4
    return jax.shard_map(
        fused if small else general,
        mesh=mesh,
        in_specs=(P(("groups", "ex"), "coord"), P("groups"), P("groups")),
        out_specs=(P("coord", ("groups", "ex")), P(("groups", "coord"), "ex")),
        check_vma=False,
    )
```

```python
import functools
import math

import jax
import jax.numpy as jnp
import numpy as np
from jax import lax
from jax.experimental import pallas as pl
from jax.experimental.pallas import tpu as pltpu
from jax.sharding import PartitionSpec as P

FEATS = 8192
LAST = int(np.array((1274126177 << 6) & 0xFFFFFFFF, np.uint32).astype(np.int32))


def sign_tile(coord_term, feat_term):
    m = coord_term ^ feat_term
    m = m ^ lax.shift_right_logical(m, jnp.int32(15))
    m = m * jnp.int32(73244475)
    m = m ^ lax.shift_right_logical(m, jnp.int32(13))
    p = m * jnp.int32(LAST)
    p = p ^ (p << 16)
    return jnp.where(p < 0, -1.0, 1.0).astype(jnp.bfloat16)


def project_kernel(sub, feat_rows, block, salt_ref, first_ref, place_ref, grads_ref, out_ref, signs, coord_term):
    coords = grads_ref.shape[1]
    step = pl.program_id(0)

    @pl.when(step == 0)
    def _():
        ids = first_ref[0] + lax.broadcasted_iota(jnp.int32, (16, coords), 1)
        coord_term[...] = (ids * 2654435) ^ salt_ref[0]

    @pl.loop(0, block // 16)
    def _(i):
        row = step * block + i * 16
        feat = (row // sub) * feat_rows + place_ref[0] * sub + row % sub
        feat_term = (feat + lax.broadcasted_iota(jnp.int32, (16, 128), 0)) * 97001
        for j in range(coords // 128):
            signs[pl.ds(pl.multiple_of(i * 16, 16), 16), pl.ds(j * 128, 128)] = sign_tile(
                coord_term[:, pl.ds(j * 128, 128)], feat_term
            )

    out_ref[...] = lax.dot_general(
        signs[...], grads_ref[...], (((1,), (1,)), ((), ())), preferred_element_type=jnp.float32
    ).astype(out_ref.dtype)


def project(gathered, salt, first, place, rows, sub, feat_rows):
    examples, coords = gathered.shape
    block = 512
    return pl.pallas_call(
        functools.partial(project_kernel, sub, feat_rows, block),
        grid=(rows // block,),
        out_shape=jax.ShapeDtypeStruct((rows, examples), jnp.bfloat16),
        in_specs=[pl.BlockSpec(memory_space=pltpu.SMEM)] * 3
        + [pl.BlockSpec((examples, coords), lambda i: (0, 0))],
        out_specs=pl.BlockSpec((block, examples), lambda i: (i, 0)),
        scratch_shapes=[
            pltpu.VMEM((block, coords), jnp.bfloat16),
            pltpu.VMEM((16, coords), jnp.int32),
        ],
        compiler_params=pltpu.CompilerParams(vmem_limit_bytes=40 * 2**20),
    )(salt, first, place, gathered)


def general(gradients, hash_salt, slab_offset):
    coord_local = gradients.shape[1]
    coord_parts = lax.axis_size("coord")
    ex_parts = lax.axis_size("ex")
    examples = gradients.shape[0] * ex_parts
    ex_local = gradients.shape[0]
    feat_rows = FEATS // coord_parts
    sub = feat_rows // ex_parts
    first = slab_offset + lax.axis_index("coord") * coord_local
    place = lax.axis_index("ex").reshape(1)
    gathered = lax.all_gather(gradients, "ex", axis=0, tiled=True)
    part = project(gathered, hash_salt, first, place, FEATS // ex_parts, sub, feat_rows)
    parts = lax.all_to_all(part.reshape(coord_parts, sub, examples), "coord", 0, 0)
    sums = jnp.sum(parts.astype(jnp.float32), axis=0)
    own = (sums / math.sqrt(coord_local * coord_parts)).astype(jnp.bfloat16)
    blocks = own.reshape(sub, ex_parts, ex_local).transpose(1, 0, 2)
    features = lax.all_to_all(blocks, "ex", 0, 0).reshape(feat_rows, ex_local)
    gram = lax.dot_general(own, own, (((0,), (0,)), ((), ())), preferred_element_type=jnp.float32) / FEATS
    gram = gram.astype(jnp.bfloat16).reshape(examples, ex_parts, ex_local).transpose(1, 0, 2)
    gram = jnp.sum(lax.all_to_all(gram, "ex", 0, 0).astype(jnp.float32), axis=0)
    gram = gram.astype(jnp.bfloat16).reshape(coord_parts, examples // coord_parts, ex_local)
    kernel = jnp.sum(lax.all_to_all(gram, "coord", 0, 0).astype(jnp.float32), axis=0)
    return features, kernel


def fused_kernel(
    salt_ref, offset_ref, grads_ref, feats_ref, kern_ref,
    grads, signs, coord_term, part, part_in, own, feat, feat_in, gram, gram_sib, gram_out, gram_in,
    local, send_g, recv_g, send_p, recv_p, send_f, recv_f, send_s, recv_s, send_k, recv_k,
):
    z, x = lax.axis_index("coord"), lax.axis_index("ex")
    xc, c = x // 2, x % 2
    zz = z % 2
    z_pair, z_far = z + 1 - 2 * zz, (z + 2) % 4
    oc, oz = 1 - c, 1 - zz
    ox = 1 - xc
    n_ex, width = grads_ref.shape
    cut = n_ex // 2
    half = signs.shape[1]
    feat_rows = FEATS // 4
    sends = []

    def remote(src, dst, send, recv, zt, xt):
        return pltpu.make_async_remote_copy(
            src_ref=src, dst_ref=dst, send_sem=send, recv_sem=recv,
            device_id={"coord": zt, "ex": xt}, device_id_type=pl.DeviceIdType.MESH,
        )

    def start(*args):
        copy = remote(*args)
        copy.start()
        sends.append(copy)

    barrier = pltpu.get_barrier_semaphore()
    chip = z * 2 + xc
    greeted = [(z, xc * 2 + oc), (z, ox * 2 + oc)]
    for d in range(1, 8):
        t = (chip + d) % 8
        greeted.append((t // 2, (t % 2) * 2 + c))
    for zt, xt in greeted:
        pl.semaphore_signal(
            barrier, inc=1, device_id={"coord": zt, "ex": xt}, device_id_type=pl.DeviceIdType.MESH
        )
    ids = offset_ref[0] + (z // 2) * (2 * width) + lax.broadcasted_iota(jnp.int32, (16, 2 * width), 1)
    coord_term[...] = (ids * 2654435) ^ salt_ref[0]
    pl.semaphore_wait(barrier, 9)

    copies = []
    for n, (zt, xt, cuts) in enumerate(((z_pair, x, (0, 1)), (z, ox * 2 + c, (0, 1)), (z, xc * 2 + oc, (0, 1)))):
        for k in cuts:
            start(
                grads_ref.at[pl.ds(k * cut, cut)], grads.at[zz, xc, k, c],
                send_g.at[2 * n + k], recv_g.at[zz, xc, k, c], zt, xt,
            )
    for k in range(2):
        copy = pltpu.make_async_copy(grads_ref.at[pl.ds(k * cut, cut)], grads.at[zz, xc, k, c], local.at[k])
        copy.start()
        copies.append(copy)

    def hash_rows(low, high):
        @pl.loop(low, high)
        def _(i):
            h = i // (half // 16)
            r = i % (half // 16)
            first = ((z + 2 * h) % 4) * feat_rows + x * half + r * 16
            feat_term = (first + lax.broadcasted_iota(jnp.int32, (16, 128), 0)) * 97001
            for j in range(2 * width // 128):
                signs[h, pl.ds(pl.multiple_of(r * 16, 16), 16), pl.ds(j * 128, 128)] = sign_tile(
                    coord_term[:, pl.ds(j * 128, 128)], feat_term
                )

    def arrived(a, b, k, core):
        slot = grads.at[a, b, k, core]
        remote(slot, slot, send_g.at[0], recv_g.at[a, b, k, core], z_pair, x).wait_recv()

    def pass_on(a, b, k, n, zt, xt):
        slot = grads.at[a, b, k, c]
        start(slot, slot, send_g.at[n], recv_g.at[a, b, k, c], zt, xt)

    def forward(a, b, k, n):
        pass_on(a, b, k, n, z, xc * 2 + oc)

    def sums(b, k, h):
        total = None
        for a in range(2):
            one = lax.dot_general(
                grads[a, b, k].reshape(n_ex, width), signs[h, :, pl.ds(a * width, width)],
                (((1,), (1,)), ((), ())), preferred_element_type=jnp.float32,
            )
            total = one if total is None else total + one
        return total

    def exchange(n):
        return remote(part.at[n], part_in.at[n], send_p.at[n], recv_p.at[n], z_far, x)

    def give(n, b, k):
        arrived(zz, b, k, oc)
        arrived(oz, b, k, oc)
        part[n] = sums(b, k, 1).astype(jnp.bfloat16)
        copy = exchange(n)
        copy.start()
        sends.append(copy)

    steps = half // 16
    hash_rows(steps, 2 * steps)
    for copy in copies:
        copy.wait()
    arrived(oz, xc, 0, c)
    pass_on(oz, xc, 0, 6, z, ox * 2 + c)
    forward(oz, xc, 0, 8)
    give(0, xc, 0)
    hash_rows(0, steps // 2)
    arrived(oz, xc, 1, c)
    pass_on(oz, xc, 1, 7, z, ox * 2 + c)
    forward(oz, xc, 1, 10)
    give(1, xc, 1)
    arrived(zz, ox, 0, c)
    forward(zz, ox, 0, 11)
    arrived(zz, ox, 1, c)
    forward(zz, ox, 1, 9)
    hash_rows(steps // 2, steps)
    arrived(oz, ox, 0, c)
    forward(oz, ox, 0, 12)
    give(2, ox, 0)
    arrived(oz, ox, 1, c)
    forward(oz, ox, 1, 13)
    give(3, ox, 1)
    chunks = ((xc, 0), (xc, 1), (ox, 0), (ox, 1))
    for n, (b, k) in enumerate(chunks):
        own[n] = sums(b, k, 0)

    for n, (b, k) in enumerate(chunks):
        exchange(n).wait_recv()
        done = (own[n] + part_in[n].astype(jnp.float32)) / math.sqrt(4 * width)
        feat[b, :, pl.ds(k * cut, cut)] = done.astype(jnp.bfloat16).reshape(2, cut, half)
        rows = pl.ds(k * cut, cut)
        into = feat_in.at[x, rows]
        if n < 2:
            start(feat.at[xc, oc, rows], into, send_f.at[0, k], recv_f.at[x, k], z, xc * 2 + oc)
        else:
            start(feat.at[ox, c, rows], into, send_f.at[1, k], recv_f.at[x, k], z, ox * 2 + c)
            start(feat.at[ox, oc, rows], into, send_f.at[2, k], recv_f.at[x, k], z, ox * 2 + oc)

    everyone = feat[...].reshape(4 * n_ex, half)

    def blocks(core):
        for b in range(2):
            block = lax.dot_general(
                everyone, feat[b, core], (((1,), (1,)), ((), ())), preferred_element_type=jnp.float32
            ) / FEATS
            for row in range(4):
                gram[core, row * 2 + b] = block[row * n_ex:(row + 1) * n_ex].astype(jnp.bfloat16)

    blocks(oc)
    sibling = remote(gram.at[oc], gram_sib, send_s, recv_s, z, xc * 2 + oc)
    sibling.start()
    sends.append(sibling)
    blocks(c)
    feat_in[x] = feat[xc, c]
    sibling.wait_recv()
    gram_out[...] = (gram[c].astype(jnp.float32) + gram_sib[...].astype(jnp.float32)).astype(jnp.bfloat16)
    for d in range(1, 8):
        t = (chip + d) % 8
        start(
            gram_out.at[t], gram_in.at[chip], send_k.at[d], recv_k.at[chip], t // 2, (t % 2) * 2 + c
        )

    for d in range(4):
        t = (x + d) % 4
        if d:
            for k in range(2):
                slot = feat_in.at[t, pl.ds(k * cut, cut)]
                remote(slot, slot, send_f.at[0, k], recv_f.at[t, k], z, t).wait_recv()
        feats_ref[:, pl.ds(pl.multiple_of(t * half, half), half)] = feat_in[t]

    total = gram[c, chip].astype(jnp.float32) + gram_sib[chip].astype(jnp.float32)
    for d in range(1, 8):
        t = (chip + d) % 8
        remote(
            gram_in.at[t], gram_in.at[t], send_k.at[0], recv_k.at[t], t // 2, (t % 2) * 2 + c
        ).wait_recv()
        total = total + gram_in[t].astype(jnp.float32)
    kern_ref[...] = total
    for copy in sends:
        copy.wait_send()


def fused(gradients, hash_salt, slab_offset):
    n_ex, width = gradients.shape
    half = FEATS // 16
    dma = pltpu.SemaphoreType.DMA
    flipped, kernel = pl.pallas_call(
        fused_kernel,
        out_shape=(
            jax.ShapeDtypeStruct((n_ex, FEATS // 4), jnp.bfloat16),
            jax.ShapeDtypeStruct((n_ex, n_ex), jnp.float32),
        ),
        in_specs=[pl.BlockSpec(memory_space=pltpu.SMEM)] * 2 + [pl.BlockSpec(memory_space=pltpu.HBM)],
        out_specs=(pl.BlockSpec(memory_space=pltpu.VMEM),) * 2,
        scratch_shapes=[
            pltpu.VMEM((2, 2, 2, 2, n_ex // 2, width), jnp.bfloat16),
            pltpu.VMEM((2, half, 2 * width), jnp.bfloat16),
            pltpu.VMEM((16, 2 * width), jnp.int32),
            pltpu.VMEM((4, n_ex, half), jnp.bfloat16),
            pltpu.VMEM((4, n_ex, half), jnp.bfloat16),
            pltpu.VMEM((4, n_ex, half), jnp.float32),
            pltpu.VMEM((2, 2, n_ex, half), jnp.bfloat16),
            pltpu.VMEM((4, n_ex, half), jnp.bfloat16),
            pltpu.VMEM((2, 8, n_ex, n_ex), jnp.bfloat16),
            pltpu.VMEM((8, n_ex, n_ex), jnp.bfloat16),
            pltpu.VMEM((8, n_ex, n_ex), jnp.bfloat16),
            pltpu.VMEM((8, n_ex, n_ex), jnp.bfloat16),
            dma((2,)), dma((14,)), dma((2, 2, 2, 2)),
            dma((4,)), dma((4,)),
            dma((3, 2)), dma((4, 2)),
            dma, dma,
            dma((8,)), dma((8,)),
        ],
        compiler_params=pltpu.CompilerParams(
            collective_id=0, has_side_effects=True, vmem_limit_bytes=48 * 2**20
        ),
    )(hash_salt, slab_offset, gradients)
    return flipped.T, kernel


def solution(mesh):
    small = mesh.shape["coord"] == 4 and mesh.shape["ex"] == 4
    return jax.shard_map(
        fused if small else general,
        mesh=mesh,
        in_specs=(P(("groups", "ex"), "coord"), P("groups"), P("groups")),
        out_specs=(P("coord", ("groups", "ex")), P(("groups", "coord"), "ex")),
        check_vma=False,
    )
```
